32 devices in a mesh: groups: 2 (over x), patch: 16 (over z, y, core).
Axes of the slice: x: 2, y: 2, z: 4, core: 2. Of those that a mesh axis runs over, the one named last changes fastest.
Arguments:
- queries: bfloat16 [4096, 384], P(('groups', 'patch')), parts along dimension 0, may hold values from -112 to 112
- fresh_kv: bfloat16 [2, 4096, 384], P(None, ('groups', 'patch')), parts along dimension 1, may hold values from -4 to 4
- stale_kv: bfloat16 [2, 4096, 384], P(None, 'groups'), parts along dimension 1, may hold values from -4 to 4
- basis_table: float32 [8, 3, 128, 16], replicated, may hold values from -0.5 to 0.5
- token_of_row: int32 [4096], P(('groups', 'patch')), parts along dimension 0, may hold values from 0 to 2047, each once
- step_index: int32 [2], P('groups'), parts along dimension 0, may hold values from 0 to 7
Outputs:
- attended: bfloat16 [4096, 384], P(('groups', 'patch')), parts along dimension 0
The draws below stay inside these ranges and needn't reach their ends.
There are 2 independent parts, one for each index of `groups`. The reference program is written for one: setup_inputs(seed, part) draws one part's arguments, and reference() takes and returns one part's arrays. A program takes and returns all parts, laid end to end along the dimension named above; an argument that names none is the same for every part. Nothing has to cross between parts.
Inputs may be any that keep to these rules, and one draw needn't show every extreme that they name: `token_of_row`: each token appears once.
All inputs are finite; a program needn't handle non-finite values.
Results may differ from the reference program's by a relative error of at most 0.0012.
Values sent between devices are 32-bit elements; how exact they have to be, the bound alone decides.
A program may use at most 192 MiB of HBM per device.

```python
import jax
import jax.numpy as jnp
from jax import lax

HEADS = 3
HEAD_DIM = 128
RANK = 16
STEPS = 8
TOKENS = 2048


def shared_rows(key):
    return jax.random.truncated_normal(key, -4.0, 4.0, (2, TOKENS, HEADS * HEAD_DIM), jnp.float32)


def draw_stale_kv(key, part):
    stale_rows = shared_rows(key)
    return stale_rows.astype(jnp.bfloat16)


def draw_queries(key, part):
    key = jax.random.fold_in(key, 5)
    query_rows = 1.6 * jax.random.truncated_normal(key, -6.25, 6.25, (TOKENS, HEADS * HEAD_DIM), jnp.float32)
    return query_rows.astype(jnp.bfloat16)


def draw_step_index(key, part):
    key = jax.random.fold_in(key, 7)
    base_step = jax.random.randint(key, (1,), 0, STEPS, jnp.int32)
    return ((base_step + 11 * part) % STEPS).astype(jnp.int32)


def steps_of(own_key, dims, pieces, low, top_value):
    gain = 1.0
    for axis_at, shards_of in pieces:
        steps = jax.random.uniform(jax.random.fold_in(jax.random.fold_in(own_key, 6), axis_at), (shards_of,), jnp.float32, low / len(pieces), top_value / len(pieces))
        gain = gain * jnp.repeat(jnp.exp(steps), dims[axis_at] // shards_of).reshape((-1,) + (1,) * (len(dims) - 1 - axis_at))
    return gain


def scatter_about(key, dims, width, limit, shards=(), dtype=jnp.bfloat16):
    level = steps_of(key, dims, shards, -0.22, 0.18) if shards else 1.0
    entries = jax.random.normal(key, dims, jnp.float32) * width * level
    return jnp.minimum(jnp.maximum(entries, -limit), limit).astype(dtype)


def setup_inputs(seed: int = 0, part: int = 0) -> dict:
    arg_keys = jax.random.split(jax.random.key(seed), 7)
    part_splits = jax.random.split(jax.random.fold_in(arg_keys[6], part), 7)
    return {
        "queries": draw_queries(jax.random.fold_in(jax.random.fold_in(arg_keys[6], part), 71), part),
        "fresh_kv": scatter_about(part_splits[1], (2, TOKENS, HEADS * HEAD_DIM), 1.0, 4.0, ((1, 16),)),
        "stale_kv": draw_stale_kv(jax.random.fold_in(jax.random.fold_in(arg_keys[6], part), 71), part),
        "basis_table": scatter_about(arg_keys[3], (STEPS, HEADS, HEAD_DIM, RANK), HEAD_DIM ** -0.5, 0.5, (), jnp.float32),
        "token_of_row": jax.random.permutation(part_splits[4], TOKENS).astype(jnp.int32),
        "step_index": draw_step_index(jax.random.fold_in(jax.random.fold_in(arg_keys[6], part), 71), part),
    }


TOP_PRECISION = lax.Precision.HIGHEST


def reference(queries, fresh_kv, stale_kv, basis_table, token_of_row, step_index):
    row_count = queries.shape[0]
    step_basis = lax.dynamic_index_in_dim(basis_table, step_index[0].astype(jnp.int32), 0, keepdims=False)
    own_stale = jnp.take(stale_kv, token_of_row.astype(jnp.int32), axis=1).astype(jnp.float32)
    residual = (fresh_kv.astype(jnp.float32) - own_stale).reshape(2, row_count, HEADS, HEAD_DIM)
    coeffs = jnp.einsum("ethd,hdr->ethr", residual, step_basis, precision=TOP_PRECISION)
    rebuilt = jnp.einsum("ethr,hdr->ethd", coeffs, step_basis, precision=TOP_PRECISION)
    refreshed = own_stale + rebuilt.reshape(2, row_count, HEADS * HEAD_DIM)
    query_heads = queries.astype(jnp.float32).reshape(row_count, HEADS, HEAD_DIM).transpose(1, 0, 2)
    key_heads = refreshed[0].reshape(row_count, HEADS, HEAD_DIM).transpose(1, 0, 2)
    value_heads = refreshed[1].reshape(row_count, HEADS, HEAD_DIM).transpose(1, 0, 2)

    def one_head(operands):
        head_query, head_keys, head_values = operands
        scores = jnp.dot(head_query, head_keys.T, precision=TOP_PRECISION) * (HEAD_DIM ** -0.5)
        shifted = jnp.exp(scores - jnp.max(scores, axis=1, keepdims=True))
        weights = shifted / jnp.sum(shifted, axis=1, keepdims=True)
        return jnp.dot(weights, head_values, precision=TOP_PRECISION)

    result = lax.map(one_head, (query_heads, key_heads, value_heads))
    return result.transpose(1, 0, 2).reshape(row_count, HEADS * HEAD_DIM).astype(jnp.bfloat16)
```

```python
import functools
import math

import jax
import jax.numpy as jnp
from jax import lax
from jax.experimental import pallas as pl
from jax.experimental.pallas import tpu as pltpu
from jax.sharding import PartitionSpec as P

MESH = pl.DeviceIdType.MESH
TOP = lax.Precision.HIGHEST
F32 = jnp.float32
BF16 = jnp.bfloat16


def dot_nn(a, b, precision=None):
    return lax.dot_general(
        a, b, (((1,), (0,)), ((), ())), precision=precision, preferred_element_type=F32
    )


def dot_nt(a, b, precision=None):
    return lax.dot_general(
        a, b, (((1,), (1,)), ((), ())), precision=precision, preferred_element_type=F32
    )


def split_parts(x, count):
    parts = []
    for _ in range(count):
        part = x.astype(BF16)
        parts.append(part)
        x = x - part.astype(F32)
    return parts


def kernel(
    span,
    tile,
    q_hbm,
    fresh_hbm,
    stale_hbm,
    basis_hbm,
    tok_hbm,
    step_hbm,
    out_ref,
    q_v,
    fresh_v,
    stale_v,
    basis_v,
    tok_v,
    step_s,
    blocks,
    scores,
    spread,
    in_sem,
    send_sem,
    recv_sem,
):
    heads, rank, head_dim = basis_v.shape[1:]
    rows = q_v.shape[0]
    tokens = stale_v.shape[1]
    coef_rows = 2 * heads * rank
    group = lax.axis_index("groups")
    me = lax.axis_index("patch")
    far, near, core = me // 4, (me % 4) // 2, me % 2
    far_peers = [(group, ((far + d) % span) * 4 + near * 2 + core) for d in range(1, span)]
    near_peer = (group, far * 4 + (1 - near) * 2 + core)
    core_peer = (group, far * 4 + near * 2 + (1 - core))

    barrier = pltpu.get_barrier_semaphore()
    for peer in far_peers + [near_peer, core_peer]:
        pl.semaphore_signal(barrier, inc=1, device_id=peer, device_id_type=MESH)

    pairs = [
        (basis_hbm, basis_v),
        (fresh_hbm, fresh_v),
        (tok_hbm, tok_v),
        (q_hbm, q_v),
        (stale_hbm.at[0], stale_v.at[0]),
        (stale_hbm.at[1], stale_v.at[1]),
        (step_hbm, step_s),
    ]
    loads = [pltpu.make_async_copy(s, d, in_sem.at[n]) for n, (s, d) in enumerate(pairs)]
    for load in loads:
        load.start()

    def send(src, dst, peer):
        return pltpu.make_async_remote_copy(
            src_ref=blocks.at[src],
            dst_ref=blocks.at[dst],
            send_sem=send_sem.at[dst],
            recv_sem=recv_sem.at[dst],
            device_id=peer,
            device_id_type=MESH,
        )

    far_sends = [send(0, d, far_peers[d - 1]) for d in range(1, span)]
    near_sends = [send(d, span + d, near_peer) for d in range(span)]
    core_sends = [send(s, 2 * span + s, core_peer) for s in range(2 * span)]

    loads[6].wait()
    loads[0].wait()
    basis = basis_v[step_s[0]]
    basis_t = [basis[h] for h in range(heads)]
    basis_parts = [split_parts(b, 3) for b in basis_t]
    loads[1].wait()
    fresh = fresh_v[...].reshape(2 * rows, heads * head_dim)
    for h in range(heads):
        cols = slice(h * head_dim, (h + 1) * head_dim)
        three = dot_nt(jnp.concatenate(basis_parts[h], axis=0), fresh[:, cols])
        coeffs = three[:rank] + three[rank : 2 * rank] + three[2 * rank :]
        for e in range(2):
            low = (e * heads + h) * rank
            blocks[0, low : low + rank, :] = coeffs[:, e * rows : (e + 1) * rows]
    loads[2].wait()
    blocks[0, coef_rows : coef_rows + 8, :] = jnp.broadcast_to(tok_v[...].astype(F32), (8, rows))

    pl.semaphore_wait(barrier, span + 1)
    for copy in far_sends:
        copy.start()
    near_sends[0].start()
    core_sends[0].start()

    loads[3].wait()
    scale = head_dim ** (-0.5) * math.log2(math.e)
    lane = lax.broadcasted_iota(jnp.int32, (rows, 5 * rank), 1)
    wide_parts, query_parts = [], []
    for h in range(heads):
        head_query = q_v[:, h * head_dim : (h + 1) * head_dim]
        wide = jnp.zeros((rows, 5 * rank), F32)
        for part in reversed(basis_parts[h]):
            wide = wide + dot_nt(head_query, jnp.concatenate([part] * 5, axis=0))
        left = head_query.astype(F32) - dot_nn(wide[:, :rank], basis_t[h], TOP)
        query_parts.append(jnp.concatenate(split_parts(left * scale, 2), axis=0))
        p1, p2, p3 = split_parts(wide * scale, 3)
        picked = jnp.where(
            lane < 2 * rank,
            p1.astype(F32),
            jnp.where(lane < 4 * rank, p2.astype(F32), p3.astype(F32)),
        )
        wide_parts.append(picked.astype(BF16))

    def stale_scores(h):
        cols = slice(h * head_dim, (h + 1) * head_dim)
        for low in range(0, tokens, tile):
            both = dot_nt(query_parts[h], stale_v[0, low : low + tile, cols])
            scores[h, :, low : low + tile] = both[:rows] + both[rows:]

    place_tile = 512

    def place(slots, first):
        lefts, columns = [], []
        for slot in slots:
            parts = split_parts(blocks[slot, :coef_rows, :], 2)
            lefts.append(jnp.concatenate(parts, axis=0))
            tok = blocks[slot, coef_rows : coef_rows + 1, :]
            columns.append(jnp.broadcast_to(tok, (rows, rows)).T)
        left = jnp.concatenate(lefts, axis=1)
        column = jnp.concatenate(columns, axis=0)
        ids = lax.broadcasted_iota(jnp.int32, (column.shape[0], rows), 1).astype(F32)
        shifted = column - ids

        def step(low):
            hots = [
                jnp.where(shifted == float(low + at), 1.0, 0.0).astype(BF16)
                for at in range(0, place_tile, rows)
            ]
            got = dot_nn(left, jnp.concatenate(hots, axis=1))
            if first:
                spread[:, low : low + place_tile] = got
            else:
                spread[:, low : low + place_tile] += got

        for low in range(0, tokens, place_tile):
            step(low)

    def place_all(base, first):
        for at in range(0, span, 4):
            place(range(base + at, base + at + 4), first and at == 0)

    loads[4].wait()
    stale_scores(0)
    for d in range(1, span):
        far_sends[d - 1].wait_recv()
        near_sends[d].start()
        core_sends[d].start()
    for h in range(1, heads):
        stale_scores(h)
    place_all(0, True)
    for d in range(span):
        near_sends[d].wait_recv()
        core_sends[span + d].start()
    for s in range(span):
        core_sends[s].wait_recv()
    place_all(2 * span, False)
    place_all(span, False)
    for s in range(span, 2 * span):
        core_sends[s].wait_recv()
    place_all(3 * span, False)

    loads[5].wait()
    lo_base = coef_rows
    for h in range(heads):
        cols = slice(h * head_dim, (h + 1) * head_dim)
        key_low, value_low = h * rank, (heads + h) * rank
        top = jnp.full((rows, 1), -jnp.inf, F32)
        for low in range(0, tokens, tile):
            span_t = slice(low, low + tile)
            key_hi = spread[key_low : key_low + rank, span_t].astype(BF16)
            key_lo = spread[lo_base + key_low : lo_base + key_low + rank, span_t].astype(BF16)
            right = jnp.concatenate([key_hi, key_lo, key_hi, key_lo, key_hi], axis=0)
            full = scores[h, :, span_t] + dot_nn(wide_parts[h], right)
            scores[h, :, span_t] = full
            top = jnp.maximum(top, jnp.max(full, axis=1, keepdims=True))
        total = jnp.zeros((rows, 1), F32)
        direct = jnp.zeros((2 * rows, head_dim), F32)
        through = jnp.zeros((2 * rows, 2 * rank), F32)
        for low in range(0, tokens, tile):
            span_t = slice(low, low + tile)
            weights = jnp.exp2(scores[h, :, span_t] - top)
            total = total + jnp.sum(weights, axis=1, keepdims=True)
            both = jnp.concatenate(split_parts(weights, 2), axis=0)
            direct = direct + dot_nn(both, stale_v[1, span_t, cols])
            value_hi = spread[value_low : value_low + rank, span_t].astype(BF16)
            value_lo = spread[lo_base + value_low : lo_base + value_low + rank, span_t].astype(BF16)
            through = through + dot_nt(both, jnp.concatenate([value_hi, value_lo], axis=0))
        direct = direct[:rows] + direct[rows:]
        through = through[:rows] + through[rows:]
        own = dot_nt(direct, basis_t[h], TOP)
        twice = jnp.concatenate([basis_t[h], basis_t[h]], axis=0)
        result = direct + dot_nn(through, twice, TOP) - dot_nn(own, basis_t[h], TOP)
        out_ref[:, cols] = (result / total).astype(out_ref.dtype)

    for copy in far_sends + near_sends + core_sends:
        copy.wait_send()


def local(span, queries, fresh_kv, stale_kv, basis_table, token_of_row, step_index):
    steps, heads, head_dim, rank = basis_table.shape
    rows, width = queries.shape
    tokens = stale_kv.shape[1]
    tile = min(tokens, 2048)
    block_rows = 2 * heads * rank + 8
    anywhere = pl.BlockSpec(memory_space=pl.ANY)
    return pl.pallas_call(
        functools.partial(kernel, span, tile),
        out_shape=jax.ShapeDtypeStruct((rows, width), BF16),
        in_specs=[anywhere] * 6,
        out_specs=pl.BlockSpec(memory_space=pltpu.VMEM),
        scratch_shapes=[
            pltpu.VMEM((rows, width), BF16),
            pltpu.VMEM((2, rows, width), BF16),
            pltpu.VMEM((2, tokens, width), BF16),
            pltpu.VMEM((steps, heads, rank, head_dim), F32),
            pltpu.VMEM((1, rows), jnp.int32),
            pltpu.SMEM((1,), jnp.int32),
            pltpu.VMEM((4 * span, block_rows, rows), F32),
            pltpu.VMEM((heads, rows, tokens), F32),
            pltpu.VMEM((4 * heads * rank, tokens), F32),
            pltpu.SemaphoreType.DMA((7,)),
            pltpu.SemaphoreType.DMA((4 * span,)),
            pltpu.SemaphoreType.DMA((4 * span,)),
        ],
        compiler_params=pltpu.CompilerParams(
            collective_id=0, has_side_effects=True, vmem_limit_bytes=60 * 1024 * 1024
        ),
        name="refreshed_attention",
    )(
        queries,
        fresh_kv,
        stale_kv,
        jnp.swapaxes(basis_table, 2, 3),
        token_of_row.reshape(1, rows),
        step_index,
    )


def solution(mesh):
    in_specs = (
        P(("groups", "patch"), None),
        P(None, ("groups", "patch"), None),
        P(None, "groups", None),
        P(),
        P(("groups", "patch")),
        P("groups"),
    )
    out_specs = P(("groups", "patch"), None)
    span = mesh.shape["patch"] // 4
    return jax.shard_map(
        functools.partial(local, span),
        mesh=mesh,
        in_specs=in_specs,
        out_specs=out_specs,
        check_vma=False,
    )
```

```python
import functools
import math

import jax
import jax.numpy as jnp
from jax import lax
from jax.experimental import pallas as pl
from jax.experimental.pallas import tpu as pltpu
from jax.sharding import PartitionSpec as P

MESH = pl.DeviceIdType.MESH
TOP = lax.Precision.HIGHEST
F32 = jnp.float32
BF16 = jnp.bfloat16


def dot_nn(a, b, precision=None):
    return lax.dot_general(
        a, b, (((1,), (0,)), ((), ())), precision=precision, preferred_element_type=F32
    )


def dot_nt(a, b, precision=None):
    return lax.dot_general(
        a, b, (((1,), (1,)), ((), ())), precision=precision, preferred_element_type=F32
    )


def split_parts(x, count):
    parts = []
    for _ in range(count):
        part = x.astype(BF16)
        parts.append(part)
        x = x - part.astype(F32)
    return parts


def kernel(
    span,
    tile,
    q_hbm,
    fresh_hbm,
    stale_hbm,
    basis_hbm,
    tok_hbm,
    step_hbm,
    out_ref,
    q_v,
    fresh_v,
    stale_v,
    basis_v,
    tok_v,
    step_s,
    blocks,
    scores,
    spread,
    in_sem,
    send_sem,
    recv_sem,
):
    heads, rank, head_dim = basis_v.shape[1:]
    rows = q_v.shape[0]
    tokens = stale_v.shape[1]
    coef_rows = 2 * heads * rank
    lanes = spread.shape[1] // 2
    group = lax.axis_index("groups")
    me = lax.axis_index("patch")
    far, near, core = me // 4, (me % 4) // 2, me % 2
    far_peers = [(group, ((far + d) % span) * 4 + near * 2 + core) for d in range(1, span)]
    near_peer = (group, far * 4 + (1 - near) * 2 + core)
    core_peer = (group, far * 4 + near * 2 + (1 - core))

    barrier = pltpu.get_barrier_semaphore()
    for peer in far_peers + [near_peer, core_peer]:
        pl.semaphore_signal(barrier, inc=1, device_id=peer, device_id_type=MESH)

    pairs = [
        (basis_hbm, basis_v),
        (fresh_hbm, fresh_v),
        (tok_hbm, tok_v),
        (q_hbm, q_v),
        (stale_hbm.at[0], stale_v.at[0]),
        (stale_hbm.at[1], stale_v.at[1]),
        (step_hbm, step_s),
    ]
    loads = [pltpu.make_async_copy(s, d, in_sem.at[n]) for n, (s, d) in enumerate(pairs)]
    for load in loads:
        load.start()

    def send(src, dst, peer):
        return pltpu.make_async_remote_copy(
            src_ref=blocks.at[src],
            dst_ref=blocks.at[dst],
            send_sem=send_sem.at[dst],
            recv_sem=recv_sem.at[dst],
            device_id=peer,
            device_id_type=MESH,
        )

    far_sends = [send(0, d, far_peers[d - 1]) for d in range(1, span)]
    near_sends = [send(d, span + d, near_peer) for d in range(span)]
    core_sends = [send(s, 2 * span + s, core_peer) for s in range(2 * span)]

    loads[6].wait()
    loads[0].wait()
    basis = basis_v[step_s[0]]
    basis_t = [basis[h] for h in range(heads)]
    basis_parts = [split_parts(b, 3) for b in basis_t]
    loads[1].wait()
    fresh = fresh_v[...].reshape(2 * rows, heads * head_dim)
    for h in range(heads):
        cols = slice(h * head_dim, (h + 1) * head_dim)
        three = dot_nt(jnp.concatenate(basis_parts[h], axis=0), fresh[:, cols])
        coeffs = three[:rank] + three[rank : 2 * rank] + three[2 * rank :]
        for e in range(2):
            low = (e * heads + h) * rank
            blocks[0, low : low + rank, :] = coeffs[:, e * rows : (e + 1) * rows]
    loads[2].wait()
    blocks[0, coef_rows : coef_rows + 8, :] = jnp.broadcast_to(tok_v[...].astype(F32), (8, rows))

    pl.semaphore_wait(barrier, span + 1)
    for copy in far_sends:
        copy.start()
    near_sends[0].start()
    core_sends[0].start()

    loads[3].wait()
    scale = head_dim ** (-0.5) * math.log2(math.e)
    half = heads * rank
    pad = lanes - 2 * half

    def at_head(part, h):
        empty = jnp.zeros((rank, head_dim), part.dtype)
        once = [part if n == h else empty for n in range(heads)]
        tail = jnp.zeros((pad, head_dim), part.dtype)
        return jnp.concatenate(once + once + [tail], axis=0)

    wide_parts, query_parts = [], []
    for h in range(heads):
        head_query = q_v[:, h * head_dim : (h + 1) * head_dim]
        placed = [at_head(part, h) for part in basis_parts[h]]
        wide = dot_nt(head_query, placed[2])
        wide = wide + dot_nt(head_query, placed[1])
        wide = wide + dot_nt(head_query, placed[0])
        back = dot_nn(wide, at_head(basis_t[h], h), TOP) * 0.5
        left = head_query.astype(F32) - back
        query_parts.append(jnp.concatenate(split_parts(left * scale, 2), axis=0))
        wide_parts.append(jnp.concatenate(split_parts(wide * scale, 2), axis=0))

    def stale_scores(h):
        cols = slice(h * head_dim, (h + 1) * head_dim)
        for low in range(0, tokens, tile):
            both = dot_nt(query_parts[h], stale_v[0, low : low + tile, cols])
            scores[h, :, low : low + tile] = both[:rows] + both[rows:]

    place_tile = 512
    one_lane = lanes + 2 * half
    ones = jnp.where(lax.broadcasted_iota(jnp.int32, (1, 2 * lanes), 1) == one_lane, 1.0, 0.0)

    def place(slots, first):
        rights, row_tokens = [], []
        for slot in slots:
            hi, lo = split_parts(blocks[slot, :coef_rows, :], 2)
            empty = jnp.zeros((pad, rows), BF16)
            rights.append(
                jnp.concatenate([hi[:half], lo[:half], empty, hi[half:], lo[half:], empty], axis=0)
            )
            row_tokens.append(blocks[slot, coef_rows : coef_rows + 1, :])
        right = jnp.concatenate(rights, axis=1)

        def step(low):
            ids = (lax.broadcasted_iota(jnp.int32, (place_tile, rows), 0) + low).astype(F32)
            hots = [jnp.where(tok == ids, 1.0, 0.0).astype(BF16) for tok in row_tokens]
            got = dot_nt(jnp.concatenate(hots, axis=1), right)
            where = pl.ds(low, place_tile)
            if first:
                spread[where, :] = (got + ones).astype(BF16)
            else:
                spread[where, :] += got.astype(BF16)

        if tokens <= 2048:
            for low in range(0, tokens, place_tile):
                step(low)
        else:

            @pl.loop(0, tokens // place_tile)
            def _(n):
                step(pl.multiple_of(n * place_tile, place_tile))

    def place_all(base, first):
        for at in range(0, span, 4):
            place(range(base + at, base + at + 4), first and at == 0)

    loads[4].wait()
    stale_scores(0)
    for d in [span - 1] + list(range(1, span - 1)):
        far_sends[d - 1].wait_recv()
        near_sends[d].start()
        core_sends[d].start()
    for h in range(1, heads):
        stale_scores(h)
    place_all(0, True)
    for s in range(span):
        core_sends[s].wait_recv()
    place_all(2 * span, False)
    for d in range(span):
        near_sends[d].wait_recv()
        core_sends[span + d].start()
    ends = []
    for h in range(heads):
        placed = [at_head(part, h) for part in basis_parts[h]]
        gram = dot_nn(basis_t[h].T, basis_t[h], TOP)
        gram_hi, gram_lo = split_parts(-gram, 2)
        ends.append(
            jnp.concatenate([gram_hi, placed[0], gram_lo, placed[1], gram_hi, placed[0]], axis=0)
        )

    place_all(span, False)
    for s in range(span, 2 * span):
        core_sends[s].wait_recv()
    place_all(3 * span, False)

    loads[5].wait()
    for h in range(heads):
        cols = slice(h * head_dim, (h + 1) * head_dim)
        top = jnp.full((rows, 1), -jnp.inf, F32)
        for low in range(0, tokens, tile):
            part = slice(low, low + tile)
            both = dot_nt(wide_parts[h], spread[part, :lanes])
            full = scores[h, :, part] + (both[:rows] + both[rows:])
            scores[h, :, part] = full
            top = jnp.maximum(top, jnp.max(full, axis=1, keepdims=True))
        mixed = jnp.zeros((2 * rows, head_dim + lanes), F32)
        for low in range(0, tokens, tile):
            part = slice(low, low + tile)
            weights = jnp.exp2(scores[h, :, part] - top)
            both = jnp.concatenate(split_parts(weights, 2), axis=0)
            right = jnp.concatenate([stale_v[1, part, cols], spread[part, lanes:]], axis=1)
            mixed = mixed + dot_nn(both, right)
        mixed = mixed[:rows] + mixed[rows:]
        total = mixed[:, head_dim + 2 * half : head_dim + 2 * half + 1]
        mixed_hi, mixed_lo = split_parts(mixed, 2)
        left = jnp.concatenate([mixed_hi, mixed_hi, mixed_lo], axis=1)
        result = mixed[:, :head_dim] + dot_nn(left, ends[h])
        out_ref[:, cols] = (result / total).astype(out_ref.dtype)

    for copy in far_sends + near_sends + core_sends:
        copy.wait_send()


def local(span, queries, fresh_kv, stale_kv, basis_table, token_of_row, step_index):
    steps, heads, head_dim, rank = basis_table.shape
    rows, width = queries.shape
    tokens = stale_kv.shape[1]
    tile = min(tokens, 2048)
    lanes = -(-(2 * heads * rank + 1) // 128) * 128
    block_rows = 2 * heads * rank + 8
    anywhere = pl.BlockSpec(memory_space=pl.ANY)
    return pl.pallas_call(
        functools.partial(kernel, span, tile),
        out_shape=jax.ShapeDtypeStruct((rows, width), BF16),
        in_specs=[anywhere] * 6,
        out_specs=pl.BlockSpec(memory_space=pltpu.VMEM),
        scratch_shapes=[
            pltpu.VMEM((rows, width), BF16),
            pltpu.VMEM((2, rows, width), BF16),
            pltpu.VMEM((2, tokens, width), BF16),
            pltpu.VMEM((steps, heads, rank, head_dim), F32),
            pltpu.VMEM((1, rows), jnp.int32),
            pltpu.SMEM((1,), jnp.int32),
            pltpu.VMEM((4 * span, block_rows, rows), F32),
            pltpu.VMEM((heads, rows, tokens), F32),
            pltpu.VMEM((tokens, 2 * lanes), BF16),
            pltpu.SemaphoreType.DMA((7,)),
            pltpu.SemaphoreType.DMA((4 * span,)),
            pltpu.SemaphoreType.DMA((4 * span,)),
        ],
        compiler_params=pltpu.CompilerParams(
            collective_id=0, has_side_effects=True, vmem_limit_bytes=60 * 1024 * 1024
        ),
        name="refreshed_attention",
    )(
        queries,
        fresh_kv,
        stale_kv,
        jnp.swapaxes(basis_table, 2, 3),
        token_of_row.reshape(1, rows),
        step_index,
    )


def solution(mesh):
    in_specs = (
        P(("groups", "patch"), None),
        P(None, ("groups", "patch"), None),
        P(None, "groups", None),
        P(),
        P(("groups", "patch")),
        P("groups"),
    )
    out_specs = P(("groups", "patch"), None)
    span = mesh.shape["patch"] // 4
    return jax.shard_map(
        functools.partial(local, span),
        mesh=mesh,
        in_specs=in_specs,
        out_specs=out_specs,
        check_vma=False,
    )
```
